32 devices in a mesh: blk: 16 (over z, x, core), partner: 2 (over y).
Axes of the slice: x: 2, y: 2, z: 4, core: 2. Of those that a mesh axis runs over, the one named last changes fastest.
Arguments:
- a_blocks: bfloat16 [16384, 3072], P(('blk', 'partner')), may hold values from -0.75 to 0.75
- p_blocks: bfloat16 [256, 4096], P(('blk', 'partner')), may hold values from -0.75 to 0.75
- agg_ids: int32 [256], P(('blk', 'partner')), may hold values from 0 to 3
- cols: int32 [256, 48], P(('blk', 'partner')), may hold values from 0 to 7
- counts: int32 [256, 8], P(('blk', 'partner')), may hold values from 0 to 6, as said below
Outputs:
- coarse: float32 [64, 64, 2048], P('blk', 'partner')
The draws below stay inside these ranges and needn't reach their ends.
Inputs may be any that keep to these rules, and one draw needn't show every extreme that they name: `cols`: a slot's row index within the device that owns its block column. `agg_ids`: an aggregate within the row's sector. The live blocks of a row for one sector offset are its first counts slots of that offset; some rows use all 6 of them.
All inputs are finite; a program needn't handle non-finite values.
Results may differ from the reference program's by a relative error of at most 0.0029.
Values may be sent and summed in bfloat16 or wider, within the bound.
A program may use at most 64 MiB of HBM per device.

```python
import jax
import jax.numpy as jnp
from jax import lax

BLOCK = 64
ROWS = 8
AGG = 4
KPER = 6
WIN = 8
SLOTS = 48
SECTORS = 16
SECTOR_ROWS = 16
FINE = 256
COARSE = 64
N_PARTNER = 2


def draw_counts(key, part):
    base_key = jax.random.fold_in(key, 11)
    start_key = jax.random.fold_in(key, 12)
    base = jax.random.randint(base_key, (FINE, WIN), 0, KPER // 2 + 1).astype(jnp.int32)
    start = jax.random.randint(start_key, (), 0, SECTORS).astype(jnp.int32)
    sector = jnp.arange(FINE, dtype=jnp.int32) // SECTOR_ROWS
    distance = (sector - start) % SECTORS
    busy = distance < max(SECTORS // 4, 1)
    return jnp.where(busy[:, None], jnp.full((FINE, WIN), KPER, jnp.int32), base).astype(jnp.int32)


def with_ends(array, stream_key, least, top_value):
    place = [jax.random.randint(jax.random.fold_in(stream_key, axis), (), 0, length) for axis, length in enumerate(array.shape)]
    longest = array.shape.index(max(array.shape))
    neighbour = place[:longest] + [(place[longest] + 1) % array.shape[longest]] + place[longest + 1:]
    return array.at[tuple(place)].set(least).at[tuple(neighbour)].set(top_value)


def levels(own_key, extent, cuts, smallest, high):
    def one(position, blocks):
        draws = jax.random.uniform(jax.random.fold_in(jax.random.fold_in(own_key, 6), position), (blocks,), jnp.float32, smallest / len(cuts), high / len(cuts))
        return jnp.repeat(jnp.exp(draws), extent[position] // blocks).reshape((-1,) + (1,) * (len(extent) - position - 1))

    gain = one(*cuts[0])
    for cut in cuts[1:]:
        gain = gain * one(*cut)
    return gain


def normal_values(rng, extent, scale, bound, pieces=(), kind=jnp.bfloat16):
    array = jax.random.normal(rng, extent, jnp.float32) * scale
    if len(pieces) > 0:
        array = levels(rng, extent, pieces, -0.22, 0.18) * array
    return jnp.clip(array, min=-bound, max=bound).astype(kind)


def setup_inputs(seed: int = 0) -> dict:
    key_of = jax.random.split(jax.random.key(seed), 6)
    a_blocks = normal_values(key_of[0], (FINE * BLOCK, SLOTS * BLOCK), BLOCK ** -0.5, 0.75, ((0, 32),))
    p_blocks = normal_values(key_of[1], (FINE, BLOCK * BLOCK), BLOCK ** -0.5, 0.75, ((0, 32),))
    agg_ids = with_ends(jax.random.randint(key_of[2], (FINE,), 0, AGG), jax.random.fold_in(key_of[2], 1), 0, AGG - 1).astype(jnp.int32)
    cols = with_ends(jax.random.randint(key_of[3], (FINE, SLOTS), 0, ROWS), jax.random.fold_in(key_of[3], 1), 0, ROWS - 1).astype(jnp.int32)
    counts = draw_counts(jax.random.fold_in(key_of[5], 71), 0)
    return {"a_blocks": a_blocks, "p_blocks": p_blocks, "agg_ids": agg_ids, "cols": cols, "counts": counts}


def indicator(labels, width):
    return (labels[..., None] == jnp.arange(width, dtype=jnp.int32)).astype(jnp.float32)


def reference(a_blocks, p_blocks, agg_ids, cols, counts):
    p_all = p_blocks.reshape(FINE, BLOCK, BLOCK)
    slot_index = jnp.arange(SLOTS, dtype=jnp.int32)
    offset_of = slot_index // KPER - WIN // 2
    window_hot = indicator(slot_index // KPER, WIN)

    def one_sector(sector):
        first = (sector * SECTOR_ROWS).astype(jnp.int32)
        row_ids = first + jnp.arange(SECTOR_ROWS, dtype=jnp.int32)
        partner_of = (row_ids // ROWS) % N_PARTNER
        target = (sector + offset_of) % SECTORS
        local_cols = lax.dynamic_slice_in_dim(cols, first, SECTOR_ROWS, 0)
        col_row = (target[None, :] * SECTOR_ROWS + partner_of[:, None] * ROWS + local_cols).astype(jnp.int32)
        count_rows = lax.dynamic_slice_in_dim(counts, first, SECTOR_ROWS, 0)
        live_mask = (slot_index[None, :] % KPER) < jnp.repeat(count_rows, KPER, axis=1)
        a_part = lax.dynamic_slice_in_dim(a_blocks, first * BLOCK, SECTOR_ROWS * BLOCK, 0)
        a_part = a_part.reshape(SECTOR_ROWS, BLOCK, SLOTS, BLOCK)
        masked = jnp.where(live_mask[:, None, :, None], a_part, jnp.zeros((), a_part.dtype))
        gathered = p_all[col_row]
        product = jnp.einsum("rasb,rsbc->rsac", masked.astype(jnp.float32), gathered.astype(jnp.float32)).astype(jnp.bfloat16)
        own_blocks = lax.dynamic_slice_in_dim(p_all, first, SECTOR_ROWS, 0)
        term_blocks = jnp.einsum("rai,rsac->rsic", own_blocks.astype(jnp.float32), product.astype(jnp.float32))
        row_agg = lax.dynamic_slice_in_dim(agg_ids, first, SECTOR_ROWS, 0)
        row_hot = indicator(row_agg, AGG)
        col_hot = indicator(agg_ids[col_row], AGG)
        col_full = col_hot[:, :, None, :] * window_hot[None, :, :, None]
        pair_hot = row_hot[:, None, :, None, None] * col_full[:, :, None, :, :]
        summed = jnp.dot(pair_hot.reshape(SECTOR_ROWS * SLOTS, AGG * WIN * AGG).T,
                         term_blocks.reshape(SECTOR_ROWS * SLOTS, BLOCK * BLOCK),
                         precision=lax.Precision.HIGHEST, preferred_element_type=jnp.float32)
        summed = summed.reshape(AGG, WIN, AGG, BLOCK, BLOCK).transpose(0, 3, 1, 2, 4)
        return summed.reshape(AGG, BLOCK, WIN * AGG * BLOCK)

    stacked = lax.map(one_sector, jnp.arange(SECTORS, dtype=jnp.int32))
    return stacked.reshape(COARSE, BLOCK, WIN * AGG * BLOCK)
```

```python
import functools

import jax
import jax.numpy as jnp
from jax import lax
from jax.experimental import pallas as pl
from jax.experimental.pallas import tpu as pltpu
from jax.sharding import PartitionSpec as P

BLOCK = 64
AGG = 4
MESH = pl.DeviceIdType.MESH
WIDE = AGG * BLOCK


def offset_of(step):
    return (1 - 2 * (step % 2)) * ((step + 1) // 2)


def kernel(n_blk, n_partner, rows, window, pairs,
           a_ref, p_ref, code_ref, out_ref,
           panels, own_t, spread, pd, parts, sent, got,
           panel_send, panel_recv, part_send, part_recv):
    me = lax.axis_index("blk")
    mine = lax.axis_index("partner")
    height = BLOCK // n_partner
    columns = rows // 2

    barrier = pltpu.get_barrier_semaphore()
    for step in range(1, window):
        source = lax.rem(me + offset_of(step) + n_blk, n_blk)
        pl.semaphore_signal(barrier, inc=1, device_id=(source, mine), device_id_type=MESH)
    for d in range(1, n_partner):
        pl.semaphore_signal(barrier, inc=1, device_id=(me, lax.rem(mine + d, n_partner)), device_id_type=MESH)
    pl.semaphore_wait(barrier, window - 1 + n_partner - 1)

    def panel_copy(step):
        return pltpu.make_async_remote_copy(
            src_ref=p_ref,
            dst_ref=panels.at[step],
            send_sem=panel_send.at[step],
            recv_sem=panel_recv.at[step],
            device_id=(lax.rem(me - offset_of(step) + n_blk, n_blk), mine),
            device_id_type=MESH,
        )

    def part_copy(step, d):
        to = lax.rem(mine + d, n_partner)
        return pltpu.make_async_remote_copy(
            src_ref=sent.at[step, to],
            dst_ref=got.at[step, d - 1],
            send_sem=part_send.at[step, d - 1],
            recv_sem=part_recv.at[step, d - 1],
            device_id=(me, to),
            device_id_type=MESH,
        )

    for step in range(1, window):
        panel_copy(step).start()

    upper = (lax.broadcasted_iota(jnp.int32, (8, 2 * BLOCK), 1) >= BLOCK).astype(jnp.float32)
    upper_row = upper[0:1]

    def place(panel):
        packed = panel[: columns * BLOCK].astype(jnp.float32)
        masks = panel[columns * BLOCK :].astype(jnp.float32)
        turned = pltpu.roll(packed, BLOCK, 1)
        for half, both in enumerate((packed * (1 - upper_row) + turned * upper_row,
                                     turned * (1 - upper_row) + packed * upper_row)):
            for column in range(columns):
                block = both[column * BLOCK : (column + 1) * BLOCK]
                row = column + half * columns
                for tile in range(2):
                    mask = masks[tile * rows + row : tile * rows + row + 1]
                    pd[row * BLOCK : (row + 1) * BLOCK, tile * 2 * BLOCK : (tile + 1) * 2 * BLOCK] = (
                        block * mask
                    ).astype(jnp.bfloat16)

    place(p_ref[...])
    own_t[...] = pd[...].astype(jnp.float32).T.astype(jnp.bfloat16)

    def one_step(step, carry):
        index = offset_of(step) + window // 2

        def one_row(g, inner):
            code = code_ref[index * rows + g]
            first = pl.multiple_of(g * BLOCK, BLOCK)
            straight = []
            for k in range(pairs):
                start = pl.multiple_of((index * pairs + k) * 2 * BLOCK, 2 * BLOCK)
                tile = a_ref[pl.ds(first, BLOCK), pl.ds(start, 2 * BLOCK)].astype(jnp.float32)
                straight.append(tile)
            tiles = straight + [pltpu.roll(tile, BLOCK, 1) for tile in straight]
            for m in range(columns):
                weight = jnp.where(code == upper + 2.0 * m, 1.0, 0.0)
                total = tiles[0] * weight[0:1]
                for r in range(1, 2 * pairs):
                    total = total + tiles[r] * weight[r : r + 1]
                spread[pl.ds(first, BLOCK), m * 2 * BLOCK : (m + 1) * 2 * BLOCK] = total.astype(jnp.bfloat16)
            return inner

        lax.fori_loop(0, rows, one_row, 0)

        @pl.when(step > 0)
        def _():
            panel_copy(step).wait_recv()
            place(panels[step])

        product = jnp.dot(spread[...], pd[...], preferred_element_type=jnp.float32)
        top = product.astype(jnp.bfloat16)
        rest = (product - top.astype(jnp.float32)).astype(jnp.bfloat16)
        coarse = jnp.dot(own_t[...], top, preferred_element_type=jnp.float32)
        coarse = coarse + jnp.dot(own_t[...], rest, preferred_element_type=jnp.float32)
        for q in range(n_partner):
            part = jnp.concatenate(
                [coarse[i * BLOCK + q * height : i * BLOCK + (q + 1) * height] for i in range(AGG)], axis=0
            )
            parts[step, q] = part
            sent[step, q] = part.astype(jnp.bfloat16)
        for d in range(1, n_partner):
            part_copy(step, d).start()
        return carry

    lax.fori_loop(0, window, one_step, 0)

    def finish(step, carry):
        index = offset_of(step) + window // 2
        total = parts[step, mine]
        for d in range(1, n_partner):
            part_copy(step, d).wait_recv()
            total = total + got[step, d - 1].astype(jnp.float32)
        start = pl.multiple_of(index * WIDE, WIDE)
        for i in range(AGG):
            out_ref[i, :, pl.ds(start, WIDE)] = total[i * height : (i + 1) * height]
        return carry

    lax.fori_loop(0, window, finish, 0)
    for step in range(1, window):
        panel_copy(step).wait_send()
    for step in range(window):
        for d in range(1, n_partner):
            part_copy(step, d).wait_send()


def on_device(n_blk, n_partner, a_blocks, p_blocks, agg_ids, cols, counts):
    rows = p_blocks.shape[0]
    window = counts.shape[1]
    kper = cols.shape[1] // window
    pairs = kper // 2
    columns = rows // 2
    height = BLOCK // n_partner
    packed = p_blocks.reshape(2, columns, BLOCK, BLOCK).transpose(1, 2, 0, 3).reshape(columns * BLOCK, 2 * BLOCK)
    lane = jnp.arange(WIDE, dtype=jnp.int32) // BLOCK
    masks = (agg_ids[None, :, None] == lane.reshape(2, 1, 2 * BLOCK)).reshape(2 * rows, 2 * BLOCK)
    panel = jnp.concatenate([packed, masks.astype(jnp.bfloat16)], axis=0)

    live = jnp.arange(kper, dtype=jnp.int32) < counts[:, :, None]
    code = jnp.where(live, cols.reshape(rows, window, kper), -4).astype(jnp.float32)
    code = code.transpose(1, 0, 2).reshape(window * rows, pairs, 2)
    code = jnp.concatenate([code, code[:, :, ::-1]], axis=1)
    code = jnp.pad(code, ((0, 0), (0, 8 - 2 * pairs), (0, 0)), constant_values=-4.0)
    code = jnp.repeat(code, BLOCK, axis=2)

    vmem = pl.BlockSpec(memory_space=pltpu.VMEM)
    size = rows * BLOCK
    return pl.pallas_call(
        functools.partial(kernel, n_blk, n_partner, rows, window, pairs),
        out_shape=jax.ShapeDtypeStruct((AGG, height, window * WIDE), jnp.float32),
        in_specs=[vmem] * 3,
        out_specs=vmem,
        scratch_shapes=[
            pltpu.VMEM((window,) + panel.shape, jnp.bfloat16),
            pltpu.VMEM((WIDE, size), jnp.bfloat16),
            pltpu.VMEM((size, size), jnp.bfloat16),
            pltpu.VMEM((size, WIDE), jnp.bfloat16),
            pltpu.VMEM((window, n_partner, AGG * height, WIDE), jnp.float32),
            pltpu.VMEM((window, n_partner, AGG * height, WIDE), jnp.bfloat16),
            pltpu.VMEM((window, max(n_partner - 1, 1), AGG * height, WIDE), jnp.bfloat16),
            pltpu.SemaphoreType.DMA((window,)),
            pltpu.SemaphoreType.DMA((window,)),
            pltpu.SemaphoreType.DMA((window, max(n_partner - 1, 1))),
            pltpu.SemaphoreType.DMA((window, max(n_partner - 1, 1))),
        ],
        compiler_params=pltpu.CompilerParams(
            collective_id=0, has_side_effects=True, vmem_limit_bytes=40 * 1024 * 1024
        ),
        cost_estimate=pl.CostEstimate(flops=3 * 10**9, bytes_accessed=5 * 10**6, transcendentals=0),
    )(a_blocks, panel, code)


def solution(mesh):
    placed = (
        P(("blk", "partner"), None),
        P(("blk", "partner"), None),
        P(("blk", "partner")),
        P(("blk", "partner"), None),
        P(("blk", "partner"), None),
    )
    return jax.shard_map(
        functools.partial(on_device, mesh.shape["blk"], mesh.shape["partner"]),
        mesh=mesh, in_specs=placed, out_specs=P("blk", "partner", None), check_vma=False,
    )
```

```python
import functools

import jax
import jax.numpy as jnp
from jax import lax
from jax.experimental import pallas as pl
from jax.experimental.pallas import tpu as pltpu
from jax.sharding import PartitionSpec as P

BLOCK = 64
AGG = 4
MESH = pl.DeviceIdType.MESH
WIDE = AGG * BLOCK


def offset_of(step):
    return (1 - 2 * (step % 2)) * ((step + 1) // 2)


def kernel(n_blk, n_partner, rows, window, kper,
           a_ref, p_ref, agg_ref, cols_ref, counts_ref, out_ref,
           a_slabs, panels, codes, raw, own_t, spread, placed, pd, parts, sent, got,
           slab_sem, panel_send, panel_recv, part_send, part_recv):
    me = lax.axis_index("blk")
    mine = lax.axis_index("partner")
    height = BLOCK // n_partner
    columns = rows // 2
    pairs = kper // 2
    wide = 2 * BLOCK
    packs = BLOCK // 2

    barrier = pltpu.get_barrier_semaphore()
    for step in range(1, window):
        source = lax.rem(me + offset_of(step) + n_blk, n_blk)
        pl.semaphore_signal(barrier, inc=1, device_id=(source, mine), device_id_type=MESH)
    for d in range(1, n_partner):
        pl.semaphore_signal(barrier, inc=1, device_id=(me, lax.rem(mine + d, n_partner)), device_id_type=MESH)

    def slab_copy(step):
        index = offset_of(step) + window // 2
        start = pl.multiple_of(index * (kper * BLOCK), wide)
        return pltpu.make_async_copy(
            a_ref.at[:, pl.ds(start, kper * BLOCK)], a_slabs.at[step], slab_sem.at[step]
        )

    for step in range(window):
        slab_copy(step).start()

    own = p_ref[...].astype(jnp.float32)
    for t in range(packs):
        raw[:, t, :] = own[:, t * wide : (t + 1) * wide]
    panels[0, : rows * packs, :] = raw[...].reshape(rows * packs, wide).astype(jnp.bfloat16)
    which = lax.broadcasted_iota(jnp.int32, (2 * rows, wide), 0)
    block_of = lax.broadcasted_iota(jnp.int32, (2 * rows, wide), 1) // BLOCK + 2 * (which // rows)
    aggregate = jnp.zeros((2 * rows, wide), jnp.int32)
    for g in range(rows):
        aggregate = jnp.where(which % rows == g, agg_ref[g], aggregate)
    panels[0, rows * packs :, :] = jnp.where(block_of == aggregate, 1.0, 0.0).astype(jnp.bfloat16)

    slots = window * kper
    for step in range(window):
        first = step * kper
        lane_slot = lax.broadcasted_iota(jnp.int32, (slots, kper * BLOCK), 1) // BLOCK
        chosen = lax.broadcasted_iota(jnp.int32, (slots, kper * BLOCK), 0) == lane_slot + first
        code = jnp.dot(cols_ref[...].astype(jnp.bfloat16), jnp.where(chosen, 1.0, 0.0).astype(jnp.bfloat16),
                       preferred_element_type=jnp.float32)
        order = lax.broadcasted_iota(jnp.int32, (rows, kper * BLOCK), 1) // BLOCK
        code = jnp.where(order < counts_ref[:, step : step + 1], code, -4.0)
        for k in range(pairs):
            straight = code[:, k * wide : (k + 1) * wide]
            for side, values in enumerate((straight, pltpu.roll(straight, BLOCK, 1))):
                for g in range(rows):
                    codes[step, g, 2 * k + side] = jnp.broadcast_to(values[g : g + 1], (8, wide))

    pl.semaphore_wait(barrier, window - 1 + n_partner - 1)

    def panel_copy(step):
        return pltpu.make_async_remote_copy(
            src_ref=panels.at[0],
            dst_ref=panels.at[step],
            send_sem=panel_send.at[step],
            recv_sem=panel_recv.at[step],
            device_id=(lax.rem(me - offset_of(step) + n_blk, n_blk), mine),
            device_id_type=MESH,
        )

    def part_copy(step, d):
        to = lax.rem(mine + d, n_partner)
        return pltpu.make_async_remote_copy(
            src_ref=sent.at[step, to],
            dst_ref=got.at[step, d - 1],
            send_sem=part_send.at[step, d - 1],
            recv_sem=part_recv.at[step, d - 1],
            device_id=(me, to),
            device_id_type=MESH,
        )

    for step in range(1, window):
        panel_copy(step).start()

    upper = (lax.broadcasted_iota(jnp.int32, (8, wide), 1) >= BLOCK).astype(jnp.float32)
    upper_row = upper[0:1]
    lower_row = 1 - upper_row

    def place(panel):
        packed = panel[: rows * packs].astype(jnp.float32)
        masks = panel[rows * packs :].astype(jnp.float32)
        turned = pltpu.roll(packed, BLOCK, 1)
        for half, both in enumerate((packed * lower_row + turned * upper_row, turned * lower_row + packed * upper_row)):
            for row in range(rows):
                block = both[row * packs : (row + 1) * packs]
                for tile in range(2):
                    mask = masks[tile * rows + row : tile * rows + row + 1]
                    placed[tile, pl.ds(row * BLOCK + half, packs, stride=2), :] = block * mask
        for tile in range(2):
            pd[:, tile * wide : (tile + 1) * wide] = placed[tile].astype(jnp.bfloat16)

    place(panels[0])
    own_t[...] = pd[...].astype(jnp.float32).T.astype(jnp.bfloat16)

    def one_step(step, carry):
        index = offset_of(step) + window // 2
        slab_copy(step).wait()

        def one_row(g, inner):
            first = pl.multiple_of(g * BLOCK, BLOCK)
            totals = [None] * columns
            for k in range(pairs):
                tile = a_slabs[step, pl.ds(first, BLOCK), k * wide : (k + 1) * wide].astype(jnp.float32)
                for side, values in enumerate((tile, pltpu.roll(tile, BLOCK, 1))):
                    code = codes[index, g, 2 * k + side]
                    grouped = values.reshape(BLOCK // 8, 8, wide)
                    for m in range(columns):
                        weight = jnp.where(code == upper + 2.0 * m, 1.0, 0.0)
                        term = grouped * weight[None]
                        totals[m] = term if totals[m] is None else totals[m] + term
            for m in range(columns):
                spread[pl.ds(first, BLOCK), m * wide : (m + 1) * wide] = (
                    totals[m].reshape(BLOCK, wide).astype(jnp.bfloat16)
                )
            return inner

        lax.fori_loop(0, rows, one_row, 0)

        @pl.when(step > 0)
        def _():
            panel_copy(step).wait_recv()
            place(panels[step])

        product = jnp.dot(spread[...], pd[...], preferred_element_type=jnp.float32)
        top = product.astype(jnp.bfloat16)
        rest = (product - top.astype(jnp.float32)).astype(jnp.bfloat16)
        coarse = jnp.dot(own_t[...], top, preferred_element_type=jnp.float32)
        coarse = coarse + jnp.dot(own_t[...], rest, preferred_element_type=jnp.float32)
        for q in range(n_partner):
            part = jnp.concatenate(
                [coarse[i * BLOCK + q * height : i * BLOCK + (q + 1) * height] for i in range(AGG)], axis=0
            )
            parts[step, q] = part
            sent[step, q] = part.astype(jnp.bfloat16)
        for d in range(1, n_partner):
            part_copy(step, d).start()
        return carry

    lax.fori_loop(0, window, one_step, 0)

    def finish(step, carry):
        index = offset_of(step) + window // 2
        total = parts[step, mine]
        for d in range(1, n_partner):
            part_copy(step, d).wait_recv()
            total = total + got[step, d - 1].astype(jnp.float32)
        start = pl.multiple_of(index * WIDE, WIDE)
        for i in range(AGG):
            out_ref[i, :, pl.ds(start, WIDE)] = total[i * height : (i + 1) * height]
        return carry

    lax.fori_loop(0, window, finish, 0)
    for step in range(1, window):
        panel_copy(step).wait_send()
    for step in range(window):
        for d in range(1, n_partner):
            part_copy(step, d).wait_send()


def on_device(n_blk, n_partner, a_blocks, p_blocks, agg_ids, cols, counts):
    rows = p_blocks.shape[0]
    window = counts.shape[1]
    kper = cols.shape[1] // window
    height = BLOCK // n_partner
    vmem = pl.BlockSpec(memory_space=pltpu.VMEM)
    size = rows * BLOCK
    others = max(n_partner - 1, 1)
    panel_rows = rows * BLOCK // 2 + 2 * rows
    return pl.pallas_call(
        functools.partial(kernel, n_blk, n_partner, rows, window, kper),
        out_shape=jax.ShapeDtypeStruct((AGG, height, window * WIDE), jnp.float32),
        in_specs=[pl.BlockSpec(memory_space=pltpu.HBM), vmem, pl.BlockSpec(memory_space=pltpu.SMEM), vmem, vmem],
        out_specs=vmem,
        scratch_shapes=[
            pltpu.VMEM((window, size, kper * BLOCK), jnp.bfloat16),
            pltpu.VMEM((window, panel_rows, 2 * BLOCK), jnp.bfloat16),
            pltpu.VMEM((window, rows, kper, 8, 2 * BLOCK), jnp.float32),
            pltpu.VMEM((rows, BLOCK // 2, 2 * BLOCK), jnp.float32),
            pltpu.VMEM((WIDE, size), jnp.bfloat16),
            pltpu.VMEM((size, size), jnp.bfloat16),
            pltpu.VMEM((2, size, 2 * BLOCK), jnp.float32),
            pltpu.VMEM((size, WIDE), jnp.bfloat16),
            pltpu.VMEM((window, n_partner, AGG * height, WIDE), jnp.float32),
            pltpu.VMEM((window, n_partner, AGG * height, WIDE), jnp.bfloat16),
            pltpu.VMEM((window, others, AGG * height, WIDE), jnp.bfloat16),
            pltpu.SemaphoreType.DMA((window,)),
            pltpu.SemaphoreType.DMA((window,)),
            pltpu.SemaphoreType.DMA((window,)),
            pltpu.SemaphoreType.DMA((window, others)),
            pltpu.SemaphoreType.DMA((window, others)),
        ],
        compiler_params=pltpu.CompilerParams(
            collective_id=0, has_side_effects=True, vmem_limit_bytes=60 * 1024 * 1024
        ),
        cost_estimate=pl.CostEstimate(flops=3 * 10**9, bytes_accessed=5 * 10**6, transcendentals=0),
    )(a_blocks, p_blocks, agg_ids, cols, counts)


def solution(mesh):
    placed = (
        P(("blk", "partner"), None),
        P(("blk", "partner"), None),
        P(("blk", "partner")),
        P(("blk", "partner"), None),
        P(("blk", "partner"), None),
    )
    return jax.shard_map(
        functools.partial(on_device, mesh.shape["blk"], mesh.shape["partner"]),
        mesh=mesh, in_specs=placed, out_specs=P("blk", "partner", None), check_vma=False,
    )
```

```python
import functools

import jax
import jax.numpy as jnp
from jax import lax
from jax.experimental import pallas as pl
from jax.experimental.pallas import tpu as pltpu
from jax.sharding import PartitionSpec as P

BLOCK = 64
AGG = 4
MESH = pl.DeviceIdType.MESH
WIDE = AGG * BLOCK


def offset_of(step):
    return (1 - 2 * (step % 2)) * ((step + 1) // 2)


def kernel(n_blk, n_partner, rows, window, kper,
           a_ref, p_ref, agg_ref, cols_ref, counts_ref, out_ref,
           a_slabs, panels, codes, raw, own_t, spread, placed, pd, parts, sent, got,
           slab_sem, panel_send, panel_recv, part_send, part_recv):
    me = lax.axis_index("blk")
    mine = lax.axis_index("partner")
    height = BLOCK // n_partner
    columns = rows // 2
    pairs = kper // 2
    wide = 2 * BLOCK
    packs = BLOCK // 2

    barrier = pltpu.get_barrier_semaphore()
    for step in range(1, window):
        source = lax.rem(me + offset_of(step) + n_blk, n_blk)
        pl.semaphore_signal(barrier, inc=1, device_id=(source, mine), device_id_type=MESH)
    for d in range(1, n_partner):
        pl.semaphore_signal(barrier, inc=1, device_id=(me, lax.rem(mine + d, n_partner)), device_id_type=MESH)

    def slab_copy(step):
        index = offset_of(step) + window // 2
        start = pl.multiple_of(index * (kper * BLOCK), wide)
        return pltpu.make_async_copy(
            a_ref.at[:, pl.ds(start, kper * BLOCK)], a_slabs.at[step], slab_sem.at[step]
        )

    for step in range(window):
        slab_copy(step).start()

    own = p_ref[...].astype(jnp.float32)
    for t in range(packs):
        raw[:, t, :] = own[:, t * wide : (t + 1) * wide]
    panels[0, : rows * packs, :] = raw[...].reshape(rows * packs, wide).astype(jnp.bfloat16)
    which = lax.broadcasted_iota(jnp.int32, (2 * rows, wide), 0)
    block_of = lax.broadcasted_iota(jnp.int32, (2 * rows, wide), 1) // BLOCK + 2 * (which // rows)
    aggregate = jnp.zeros((2 * rows, wide), jnp.int32)
    for g in range(rows):
        aggregate = jnp.where(which % rows == g, agg_ref[g], aggregate)
    panels[0, rows * packs :, :] = jnp.where(block_of == aggregate, 1.0, 0.0).astype(jnp.bfloat16)

    slots = window * kper
    for step in range(window):
        first = step * kper
        lane_slot = lax.broadcasted_iota(jnp.int32, (slots, kper * BLOCK), 1) // BLOCK
        chosen = lax.broadcasted_iota(jnp.int32, (slots, kper * BLOCK), 0) == lane_slot + first
        code = jnp.dot(cols_ref[...].astype(jnp.bfloat16), jnp.where(chosen, 1.0, 0.0).astype(jnp.bfloat16),
                       preferred_element_type=jnp.float32)
        order = lax.broadcasted_iota(jnp.int32, (rows, kper * BLOCK), 1) // BLOCK
        code = jnp.where(order < counts_ref[:, step : step + 1], code, -4.0)
        for k in range(pairs):
            straight = code[:, k * wide : (k + 1) * wide]
            for side, values in enumerate((straight, pltpu.roll(straight, BLOCK, 1))):
                for g in range(rows):
                    codes[step, g, 2 * k + side] = jnp.broadcast_to(values[g : g + 1], (8, wide))

    pl.semaphore_wait(barrier, window - 1 + n_partner - 1)

    def panel_copy(step):
        return pltpu.make_async_remote_copy(
            src_ref=panels.at[0],
            dst_ref=panels.at[step],
            send_sem=panel_send.at[step],
            recv_sem=panel_recv.at[step],
            device_id=(lax.rem(me - offset_of(step) + n_blk, n_blk), mine),
            device_id_type=MESH,
        )

    def part_copy(step, d):
        to = lax.rem(mine + d, n_partner)
        return pltpu.make_async_remote_copy(
            src_ref=sent.at[step, to],
            dst_ref=got.at[step, d - 1],
            send_sem=part_send.at[step, d - 1],
            recv_sem=part_recv.at[step, d - 1],
            device_id=(me, to),
            device_id_type=MESH,
        )

    for step in range(1, window):
        panel_copy(step).start()

    upper = (lax.broadcasted_iota(jnp.int32, (8, wide), 1) >= BLOCK).astype(jnp.float32)
    upper_row = upper[0:1]
    lower_row = 1 - upper_row

    def place(panel):
        packed = panel[: rows * packs].astype(jnp.float32)
        masks = panel[rows * packs :].astype(jnp.float32)
        turned = pltpu.roll(packed, BLOCK, 1)
        for half, both in enumerate((packed * lower_row + turned * upper_row, turned * lower_row + packed * upper_row)):
            for row in range(rows):
                block = both[row * packs : (row + 1) * packs]
                for tile in range(2):
                    mask = masks[tile * rows + row : tile * rows + row + 1]
                    placed[tile, pl.ds(row * BLOCK + half, packs, stride=2), :] = block * mask
        for tile in range(2):
            pd[:, tile * wide : (tile + 1) * wide] = placed[tile].astype(jnp.bfloat16)

    place(panels[0])
    own_t[...] = pd[...].astype(jnp.float32).T.astype(jnp.bfloat16)

    def one_step(step, carry):
        index = offset_of(step) + window // 2
        slab_copy(step).wait()

        def one_row(g, inner):
            first = pl.multiple_of(g * BLOCK, BLOCK)
            totals = [None] * columns
            for k in range(pairs):
                tile = a_slabs[step, pl.ds(first, BLOCK), k * wide : (k + 1) * wide].astype(jnp.float32)
                for side, values in enumerate((tile, pltpu.roll(tile, BLOCK, 1))):
                    code = codes[index, g, 2 * k + side]
                    grouped = values.reshape(BLOCK // 8, 8, wide)
                    for m in range(columns):
                        weight = jnp.where(code == upper + 2.0 * m, 1.0, 0.0)
                        term = grouped * weight[None]
                        totals[m] = term if totals[m] is None else totals[m] + term
            for m in range(columns):
                spread[pl.ds(first, BLOCK), m * wide : (m + 1) * wide] = (
                    totals[m].reshape(BLOCK, wide).astype(jnp.bfloat16)
                )
            return inner

        lax.fori_loop(0, rows, one_row, 0, unroll=4)

        if type(step) is not int:
            panel_copy(step).wait_recv()
            place(panels[step])

        product = jnp.dot(spread[...], pd[...], preferred_element_type=jnp.float32)
        top = product.astype(jnp.bfloat16)
        rest = (product - top.astype(jnp.float32)).astype(jnp.bfloat16)
        coarse = jnp.dot(own_t[...], top, preferred_element_type=jnp.float32)
        coarse = coarse + jnp.dot(own_t[...], rest, preferred_element_type=jnp.float32)
        for q in range(n_partner):
            part = jnp.concatenate(
                [coarse[i * BLOCK + q * height : i * BLOCK + (q + 1) * height] for i in range(AGG)], axis=0
            )
            parts[step, q] = part
            sent[step, q] = part.astype(jnp.bfloat16)
        for d in range(1, n_partner):
            part_copy(step, d).start()
        return carry

    one_step(0, 0)
    lax.fori_loop(1, window, one_step, 0)

    def finish(step, carry):
        index = offset_of(step) + window // 2
        total = parts[step, mine]
        for d in range(1, n_partner):
            part_copy(step, d).wait_recv()
            total = total + got[step, d - 1].astype(jnp.float32)
        start = pl.multiple_of(index * WIDE, WIDE)
        for i in range(AGG):
            out_ref[i, :, pl.ds(start, WIDE)] = total[i * height : (i + 1) * height]
        return carry

    lax.fori_loop(0, window, finish, 0)
    for step in range(1, window):
        panel_copy(step).wait_send()
    for step in range(window):
        for d in range(1, n_partner):
            part_copy(step, d).wait_send()


def on_device(n_blk, n_partner, a_blocks, p_blocks, agg_ids, cols, counts):
    rows = p_blocks.shape[0]
    window = counts.shape[1]
    kper = cols.shape[1] // window
    height = BLOCK // n_partner
    vmem = pl.BlockSpec(memory_space=pltpu.VMEM)
    size = rows * BLOCK
    others = max(n_partner - 1, 1)
    panel_rows = rows * BLOCK // 2 + 2 * rows
    return pl.pallas_call(
        functools.partial(kernel, n_blk, n_partner, rows, window, kper),
        out_shape=jax.ShapeDtypeStruct((AGG, height, window * WIDE), jnp.float32),
        in_specs=[pl.BlockSpec(memory_space=pltpu.HBM), vmem, pl.BlockSpec(memory_space=pltpu.SMEM), vmem, vmem],
        out_specs=vmem,
        scratch_shapes=[
            pltpu.VMEM((window, size, kper * BLOCK), jnp.bfloat16),
            pltpu.VMEM((window, panel_rows, 2 * BLOCK), jnp.bfloat16),
            pltpu.VMEM((window, rows, kper, 8, 2 * BLOCK), jnp.float32),
            pltpu.VMEM((rows, BLOCK // 2, 2 * BLOCK), jnp.float32),
            pltpu.VMEM((WIDE, size), jnp.bfloat16),
            pltpu.VMEM((size, size), jnp.bfloat16),
            pltpu.VMEM((2, size, 2 * BLOCK), jnp.float32),
            pltpu.VMEM((size, WIDE), jnp.bfloat16),
            pltpu.VMEM((window, n_partner, AGG * height, WIDE), jnp.float32),
            pltpu.VMEM((window, n_partner, AGG * height, WIDE), jnp.bfloat16),
            pltpu.VMEM((window, others, AGG * height, WIDE), jnp.bfloat16),
            pltpu.SemaphoreType.DMA((window,)),
            pltpu.SemaphoreType.DMA((window,)),
            pltpu.SemaphoreType.DMA((window,)),
            pltpu.SemaphoreType.DMA((window, others)),
            pltpu.SemaphoreType.DMA((window, others)),
        ],
        compiler_params=pltpu.CompilerParams(
            collective_id=0, has_side_effects=True, vmem_limit_bytes=60 * 1024 * 1024
        ),
        cost_estimate=pl.CostEstimate(flops=3 * 10**9, bytes_accessed=5 * 10**6, transcendentals=0),
    )(a_blocks, p_blocks, agg_ids, cols, counts)


def solution(mesh):
    placed = (
        P(("blk", "partner"), None),
        P(("blk", "partner"), None),
        P(("blk", "partner")),
        P(("blk", "partner"), None),
        P(("blk", "partner"), None),
    )
    return jax.shard_map(
        functools.partial(on_device, mesh.shape["blk"], mesh.shape["partner"]),
        mesh=mesh, in_specs=placed, out_specs=P("blk", "partner", None), check_vma=False,
    )
```

```python
import functools

import jax
import jax.numpy as jnp
from jax import lax
from jax.experimental import pallas as pl
from jax.experimental.pallas import tpu as pltpu
from jax.sharding import PartitionSpec as P

BLOCK = 64
AGG = 4
MESH = pl.DeviceIdType.MESH
WIDE = AGG * BLOCK


def offset_of(step):
    return (1 - 2 * (step % 2)) * ((step + 1) // 2)


def kernel(n_blk, n_partner, rows, window, kper,
           a_ref, p_ref, agg_ref, cols_ref, counts_ref, out_ref,
           a_slabs, panels, codes, raw, own_t, spread, placed, pd, parts, sent, got,
           slab_sem, panel_send, panel_recv, part_send, part_recv):
    me = lax.axis_index("blk")
    mine = lax.axis_index("partner")
    height = BLOCK // n_partner
    columns = rows // 2
    pairs = kper // 2
    wide = 2 * BLOCK
    packs = BLOCK // 2

    barrier = pltpu.get_barrier_semaphore()
    for step in range(1, window):
        source = lax.rem(me + offset_of(step) + n_blk, n_blk)
        pl.semaphore_signal(barrier, inc=1, device_id=(source, mine), device_id_type=MESH)
    for d in range(1, n_partner):
        pl.semaphore_signal(barrier, inc=1, device_id=(me, lax.rem(mine + d, n_partner)), device_id_type=MESH)

    def slab_copy(step):
        index = offset_of(step) + window // 2
        start = pl.multiple_of(index * (kper * BLOCK), wide)
        return pltpu.make_async_copy(
            a_ref.at[:, pl.ds(start, kper * BLOCK)], a_slabs.at[step], slab_sem.at[step]
        )

    for step in range(window):
        slab_copy(step).start()

    own = p_ref[...].astype(jnp.float32)
    for t in range(packs):
        raw[:, t, :] = own[:, t * wide : (t + 1) * wide]
    panels[0, : rows * packs, :] = raw[...].reshape(rows * packs, wide).astype(jnp.bfloat16)
    which = lax.broadcasted_iota(jnp.int32, (2 * rows, wide), 0)
    block_of = lax.broadcasted_iota(jnp.int32, (2 * rows, wide), 1) // BLOCK + 2 * (which // rows)
    aggregate = jnp.zeros((2 * rows, wide), jnp.int32)
    for g in range(rows):
        aggregate = jnp.where(which % rows == g, agg_ref[g], aggregate)
    panels[0, rows * packs :, :] = jnp.where(block_of == aggregate, 1.0, 0.0).astype(jnp.bfloat16)

    slots = window * kper
    for step in range(window):
        first = step * kper
        lane_slot = lax.broadcasted_iota(jnp.int32, (slots, kper * BLOCK), 1) // BLOCK
        chosen = lax.broadcasted_iota(jnp.int32, (slots, kper * BLOCK), 0) == lane_slot + first
        code = jnp.dot(cols_ref[...].astype(jnp.bfloat16), jnp.where(chosen, 1.0, 0.0).astype(jnp.bfloat16),
                       preferred_element_type=jnp.float32)
        order = lax.broadcasted_iota(jnp.int32, (rows, kper * BLOCK), 1) // BLOCK
        code = jnp.where(order < counts_ref[:, step : step + 1], code, -4.0)
        for k in range(pairs):
            straight = code[:, k * wide : (k + 1) * wide]
            for side, values in enumerate((straight, pltpu.roll(straight, BLOCK, 1))):
                for g in range(rows):
                    codes[step, g, 2 * k + side] = jnp.broadcast_to(values[g : g + 1], (8, wide))

    pl.semaphore_wait(barrier, window - 1 + n_partner - 1)

    def panel_copy(step):
        return pltpu.make_async_remote_copy(
            src_ref=panels.at[0],
            dst_ref=panels.at[step],
            send_sem=panel_send.at[step],
            recv_sem=panel_recv.at[step],
            device_id=(lax.rem(me - offset_of(step) + n_blk, n_blk), mine),
            device_id_type=MESH,
        )

    def part_copy(step, d):
        to = lax.rem(mine + d, n_partner)
        return pltpu.make_async_remote_copy(
            src_ref=sent.at[step, to],
            dst_ref=got.at[step, d - 1],
            send_sem=part_send.at[step, d - 1],
            recv_sem=part_recv.at[step, d - 1],
            device_id=(me, to),
            device_id_type=MESH,
        )

    for step in range(1, window):
        panel_copy(step).start()

    upper = (lax.broadcasted_iota(jnp.int32, (8, wide), 1) >= BLOCK).astype(jnp.float32)
    upper_row = upper[0:1]
    lower_row = 1 - upper_row

    def place(panel):
        packed = panel[: rows * packs].astype(jnp.float32)
        masks = panel[rows * packs :].astype(jnp.float32)
        turned = pltpu.roll(packed, BLOCK, 1)
        for half, both in enumerate((packed * lower_row + turned * upper_row, turned * lower_row + packed * upper_row)):
            for row in range(rows):
                block = both[row * packs : (row + 1) * packs]
                for tile in range(2):
                    mask = masks[tile * rows + row : tile * rows + row + 1]
                    placed[tile, pl.ds(row * BLOCK + half, packs, stride=2), :] = block * mask
        for tile in range(2):
            pd[:, tile * wide : (tile + 1) * wide] = placed[tile].astype(jnp.bfloat16)

    place(panels[0])
    own_t[...] = pd[...].astype(jnp.float32).T.astype(jnp.bfloat16)

    def one_step(step, carry):
        index = offset_of(step) + window // 2
        slab_copy(step).wait()

        def one_row(g, inner):
            first = pl.multiple_of(g * BLOCK, BLOCK)
            totals = [None] * columns
            for k in range(pairs):
                tile = a_slabs[step, pl.ds(first, BLOCK), k * wide : (k + 1) * wide].astype(jnp.float32)
                for side, values in enumerate((tile, pltpu.roll(tile, BLOCK, 1))):
                    code = codes[index, g, 2 * k + side]
                    grouped = values.reshape(BLOCK // 8, 8, wide)
                    for m in range(columns):
                        weight = jnp.where(code == upper + 2.0 * m, 1.0, 0.0)
                        term = grouped * weight[None]
                        totals[m] = term if totals[m] is None else totals[m] + term
            for m in range(columns):
                spread[pl.ds(first, BLOCK), m * wide : (m + 1) * wide] = (
                    totals[m].reshape(BLOCK, wide).astype(jnp.bfloat16)
                )
            return inner

        lax.fori_loop(0, rows, one_row, 0, unroll=4)

        if type(step) is not int:
            panel_copy(step).wait_recv()
            place(panels[step])

        product = jnp.dot(spread[...], pd[...], preferred_element_type=jnp.float32)
        top = product.astype(jnp.bfloat16)
        rest = (product - top.astype(jnp.float32)).astype(jnp.bfloat16)
        both = jnp.dot(own_t[...], jnp.concatenate([top, rest], axis=1), preferred_element_type=jnp.float32)
        coarse = both[:, :WIDE] + both[:, WIDE:]
        for q in range(n_partner):
            part = jnp.concatenate(
                [coarse[i * BLOCK + q * height : i * BLOCK + (q + 1) * height] for i in range(AGG)], axis=0
            )
            parts[step, q] = part
            sent[step, q] = part.astype(jnp.bfloat16)
        for d in range(1, n_partner):
            part_copy(step, d).start()
        return carry

    one_step(0, 0)
    lax.fori_loop(1, window, one_step, 0)

    def finish(step, carry):
        index = offset_of(step) + window // 2
        total = parts[step, mine]
        for d in range(1, n_partner):
            part_copy(step, d).wait_recv()
            total = total + got[step, d - 1].astype(jnp.float32)
        start = pl.multiple_of(index * WIDE, WIDE)
        for i in range(AGG):
            out_ref[i, :, pl.ds(start, WIDE)] = total[i * height : (i + 1) * height]
        return carry

    lax.fori_loop(0, window, finish, 0)
    for step in range(1, window):
        panel_copy(step).wait_send()
    for step in range(window):
        for d in range(1, n_partner):
            part_copy(step, d).wait_send()


def on_device(n_blk, n_partner, a_blocks, p_blocks, agg_ids, cols, counts):
    rows = p_blocks.shape[0]
    window = counts.shape[1]
    kper = cols.shape[1] // window
    height = BLOCK // n_partner
    vmem = pl.BlockSpec(memory_space=pltpu.VMEM)
    size = rows * BLOCK
    others = max(n_partner - 1, 1)
    panel_rows = rows * BLOCK // 2 + 2 * rows
    return pl.pallas_call(
        functools.partial(kernel, n_blk, n_partner, rows, window, kper),
        out_shape=jax.ShapeDtypeStruct((AGG, height, window * WIDE), jnp.float32),
        in_specs=[pl.BlockSpec(memory_space=pltpu.HBM), vmem, pl.BlockSpec(memory_space=pltpu.SMEM), vmem, vmem],
        out_specs=vmem,
        scratch_shapes=[
            pltpu.VMEM((window, size, kper * BLOCK), jnp.bfloat16),
            pltpu.VMEM((window, panel_rows, 2 * BLOCK), jnp.bfloat16),
            pltpu.VMEM((window, rows, kper, 8, 2 * BLOCK), jnp.float32),
            pltpu.VMEM((rows, BLOCK // 2, 2 * BLOCK), jnp.float32),
            pltpu.VMEM((WIDE, size), jnp.bfloat16),
            pltpu.VMEM((size, size), jnp.bfloat16),
            pltpu.VMEM((2, size, 2 * BLOCK), jnp.float32),
            pltpu.VMEM((size, WIDE), jnp.bfloat16),
            pltpu.VMEM((window, n_partner, AGG * height, WIDE), jnp.float32),
            pltpu.VMEM((window, n_partner, AGG * height, WIDE), jnp.bfloat16),
            pltpu.VMEM((window, others, AGG * height, WIDE), jnp.bfloat16),
            pltpu.SemaphoreType.DMA((window,)),
            pltpu.SemaphoreType.DMA((window,)),
            pltpu.SemaphoreType.DMA((window,)),
            pltpu.SemaphoreType.DMA((window, others)),
            pltpu.SemaphoreType.DMA((window, others)),
        ],
        compiler_params=pltpu.CompilerParams(
            collective_id=0, has_side_effects=True, vmem_limit_bytes=60 * 1024 * 1024
        ),
        cost_estimate=pl.CostEstimate(flops=3 * 10**9, bytes_accessed=5 * 10**6, transcendentals=0),
    )(a_blocks, p_blocks, agg_ids, cols, counts)


def solution(mesh):
    placed = (
        P(("blk", "partner"), None),
        P(("blk", "partner"), None),
        P(("blk", "partner")),
        P(("blk", "partner"), None),
        P(("blk", "partner"), None),
    )
    return jax.shard_map(
        functools.partial(on_device, mesh.shape["blk"], mesh.shape["partner"]),
        mesh=mesh, in_specs=placed, out_specs=P("blk", "partner", None), check_vma=False,
    )
```

```python
import functools

import jax
import jax.numpy as jnp
from jax import lax
from jax.experimental import pallas as pl
from jax.experimental.pallas import tpu as pltpu
from jax.sharding import PartitionSpec as P

BLOCK = 64
AGG = 4
MESH = pl.DeviceIdType.MESH
WIDE = AGG * BLOCK


def offset_of(step):
    return (1 - 2 * (step % 2)) * ((step + 1) // 2)


def kernel(n_blk, n_partner, rows, window, kper,
           a_ref, p_ref, agg_ref, cols_ref, counts_ref, out_ref,
           a_slabs, panels, codes, raw, own_t, spread, placed, pd, parts, sent, got,
           slab_sem, panel_send, panel_recv, part_send, part_recv):
    me = lax.axis_index("blk")
    mine = lax.axis_index("partner")
    height = BLOCK // n_partner
    columns = rows // 2
    pairs = kper // 2
    wide = 2 * BLOCK
    packs = BLOCK // 2

    barrier = pltpu.get_barrier_semaphore()
    for step in range(1, window):
        source = lax.rem(me + offset_of(step) + n_blk, n_blk)
        pl.semaphore_signal(barrier, inc=1, device_id=(source, mine), device_id_type=MESH)
    for d in range(1, n_partner):
        pl.semaphore_signal(barrier, inc=1, device_id=(me, lax.rem(mine + d, n_partner)), device_id_type=MESH)

    def slab_copy(step):
        index = offset_of(step) + window // 2
        start = pl.multiple_of(index * (kper * BLOCK), wide)
        return pltpu.make_async_copy(
            a_ref.at[:, pl.ds(start, kper * BLOCK)], a_slabs.at[step], slab_sem.at[step]
        )

    for step in range(window):
        slab_copy(step).start()

    own = p_ref[...].astype(jnp.float32)
    for t in range(packs):
        raw[:, t, :] = own[:, t * wide : (t + 1) * wide]
    panels[0, : rows * packs, :] = raw[...].reshape(rows * packs, wide).astype(jnp.bfloat16)
    which = lax.broadcasted_iota(jnp.int32, (2 * rows, wide), 0)
    block_of = lax.broadcasted_iota(jnp.int32, (2 * rows, wide), 1) // BLOCK + 2 * (which // rows)
    aggregate = jnp.zeros((2 * rows, wide), jnp.int32)
    for g in range(rows):
        aggregate = jnp.where(which % rows == g, agg_ref[g], aggregate)
    panels[0, rows * packs :, :] = jnp.where(block_of == aggregate, 1.0, 0.0).astype(jnp.bfloat16)

    slots = window * kper
    for step in range(window):
        first = step * kper
        lane_slot = lax.broadcasted_iota(jnp.int32, (slots, kper * BLOCK), 1) // BLOCK
        chosen = lax.broadcasted_iota(jnp.int32, (slots, kper * BLOCK), 0) == lane_slot + first
        code = jnp.dot(cols_ref[...].astype(jnp.bfloat16), jnp.where(chosen, 1.0, 0.0).astype(jnp.bfloat16),
                       preferred_element_type=jnp.float32)
        order = lax.broadcasted_iota(jnp.int32, (rows, kper * BLOCK), 1) // BLOCK
        code = jnp.where(order < counts_ref[:, step : step + 1], code, -4.0)
        for k in range(pairs):
            straight = code[:, k * wide : (k + 1) * wide]
            for side, values in enumerate((straight, pltpu.roll(straight, BLOCK, 1))):
                for g in range(rows):
                    codes[step, g, 2 * k + side] = jnp.broadcast_to(values[g : g + 1], (8, wide))

    pl.semaphore_wait(barrier, window - 1 + n_partner - 1)

    def panel_copy(step):
        return pltpu.make_async_remote_copy(
            src_ref=panels.at[0],
            dst_ref=panels.at[step],
            send_sem=panel_send.at[step],
            recv_sem=panel_recv.at[step],
            device_id=(lax.rem(me - offset_of(step) + n_blk, n_blk), mine),
            device_id_type=MESH,
        )

    def part_copy(step, d):
        to = lax.rem(mine + d, n_partner)
        return pltpu.make_async_remote_copy(
            src_ref=sent.at[step, to],
            dst_ref=got.at[step, d - 1],
            send_sem=part_send.at[step, d - 1],
            recv_sem=part_recv.at[step, d - 1],
            device_id=(me, to),
            device_id_type=MESH,
        )

    for step in range(1, window):
        panel_copy(step).start()

    upper = (lax.broadcasted_iota(jnp.int32, (8, wide), 1) >= BLOCK).astype(jnp.float32)
    upper_row = upper[0:1]
    lower_row = 1 - upper_row

    def place(panel):
        packed = panel[: rows * packs].astype(jnp.float32)
        masks = panel[rows * packs :].astype(jnp.float32)
        turned = pltpu.roll(packed, BLOCK, 1)
        for half, both in enumerate((packed * lower_row + turned * upper_row, turned * lower_row + packed * upper_row)):
            for row in range(rows):
                block = both[row * packs : (row + 1) * packs]
                for tile in range(2):
                    mask = masks[tile * rows + row : tile * rows + row + 1]
                    placed[tile, pl.ds(row * BLOCK + half, packs, stride=2), :] = block * mask
        for tile in range(2):
            pd[:, tile * wide : (tile + 1) * wide] = placed[tile].astype(jnp.bfloat16)

    place(panels[0])
    own_t[...] = pd[...].astype(jnp.float32).T.astype(jnp.bfloat16)

    def one_step(step, carry):
        index = offset_of(step) + window // 2
        slab_copy(step).wait()

        def one_row(g, inner):
            first = pl.multiple_of(g * BLOCK, BLOCK)
            totals = [None] * columns
            for k in range(pairs):
                tile = a_slabs[step, pl.ds(first, BLOCK), k * wide : (k + 1) * wide].astype(jnp.float32)
                for side, values in enumerate((tile, pltpu.roll(tile, BLOCK, 1))):
                    code = codes[index, g, 2 * k + side]
                    grouped = values.reshape(BLOCK // 8, 8, wide)
                    for m in range(columns):
                        weight = jnp.where(code == upper + 2.0 * m, 1.0, 0.0)
                        term = grouped * weight[None]
                        totals[m] = term if totals[m] is None else totals[m] + term
            for m in range(columns):
                spread[pl.ds(first, BLOCK), m * wide : (m + 1) * wide] = (
                    totals[m].reshape(BLOCK, wide).astype(jnp.bfloat16)
                )
            return inner

        lax.fori_loop(0, rows, one_row, 0, unroll=4)

        if type(step) is not int:
            panel_copy(step).wait_recv()
            place(panels[step])

        product = jnp.dot(spread[...], pd[...], preferred_element_type=jnp.float32)
        top = product.astype(jnp.bfloat16)
        rest = (product - top.astype(jnp.float32)).astype(jnp.bfloat16)
        coarse = jnp.dot(own_t[...], top, preferred_element_type=jnp.float32)
        coarse = coarse + jnp.dot(own_t[...], rest, preferred_element_type=jnp.float32)
        for q in range(n_partner):
            part = jnp.concatenate(
                [coarse[i * BLOCK + q * height : i * BLOCK + (q + 1) * height] for i in range(AGG)], axis=0
            )
            parts[step, q] = part
            sent[step, q] = part.astype(jnp.bfloat16)
        for d in range(1, n_partner):
            part_copy(step, d).start()
        return carry

    one_step(0, 0)
    lax.fori_loop(1, window, one_step, 0, unroll=True)

    def finish(step, carry):
        index = offset_of(step) + window // 2
        total = parts[step, mine]
        for d in range(1, n_partner):
            part_copy(step, d).wait_recv()
            total = total + got[step, d - 1].astype(jnp.float32)
        start = pl.multiple_of(index * WIDE, WIDE)
        for i in range(AGG):
            out_ref[i, :, pl.ds(start, WIDE)] = total[i * height : (i + 1) * height]
        return carry

    lax.fori_loop(0, window, finish, 0)
    for step in range(1, window):
        panel_copy(step).wait_send()
    for step in range(window):
        for d in range(1, n_partner):
            part_copy(step, d).wait_send()


def on_device(n_blk, n_partner, a_blocks, p_blocks, agg_ids, cols, counts):
    rows = p_blocks.shape[0]
    window = counts.shape[1]
    kper = cols.shape[1] // window
    height = BLOCK // n_partner
    vmem = pl.BlockSpec(memory_space=pltpu.VMEM)
    size = rows * BLOCK
    others = max(n_partner - 1, 1)
    panel_rows = rows * BLOCK // 2 + 2 * rows
    return pl.pallas_call(
        functools.partial(kernel, n_blk, n_partner, rows, window, kper),
        out_shape=jax.ShapeDtypeStruct((AGG, height, window * WIDE), jnp.float32),
        in_specs=[pl.BlockSpec(memory_space=pltpu.HBM), vmem, pl.BlockSpec(memory_space=pltpu.SMEM), vmem, vmem],
        out_specs=vmem,
        scratch_shapes=[
            pltpu.VMEM((window, size, kper * BLOCK), jnp.bfloat16),
            pltpu.VMEM((window, panel_rows, 2 * BLOCK), jnp.bfloat16),
            pltpu.VMEM((window, rows, kper, 8, 2 * BLOCK), jnp.float32),
            pltpu.VMEM((rows, BLOCK // 2, 2 * BLOCK), jnp.float32),
            pltpu.VMEM((WIDE, size), jnp.bfloat16),
            pltpu.VMEM((size, size), jnp.bfloat16),
            pltpu.VMEM((2, size, 2 * BLOCK), jnp.float32),
            pltpu.VMEM((size, WIDE), jnp.bfloat16),
            pltpu.VMEM((window, n_partner, AGG * height, WIDE), jnp.float32),
            pltpu.VMEM((window, n_partner, AGG * height, WIDE), jnp.bfloat16),
            pltpu.VMEM((window, others, AGG * height, WIDE), jnp.bfloat16),
            pltpu.SemaphoreType.DMA((window,)),
            pltpu.SemaphoreType.DMA((window,)),
            pltpu.SemaphoreType.DMA((window,)),
            pltpu.SemaphoreType.DMA((window, others)),
            pltpu.SemaphoreType.DMA((window, others)),
        ],
        compiler_params=pltpu.CompilerParams(
            collective_id=0, has_side_effects=True, vmem_limit_bytes=60 * 1024 * 1024
        ),
        cost_estimate=pl.CostEstimate(flops=3 * 10**9, bytes_accessed=5 * 10**6, transcendentals=0),
    )(a_blocks, p_blocks, agg_ids, cols, counts)


def solution(mesh):
    placed = (
        P(("blk", "partner"), None),
        P(("blk", "partner"), None),
        P(("blk", "partner")),
        P(("blk", "partner"), None),
        P(("blk", "partner"), None),
    )
    return jax.shard_map(
        functools.partial(on_device, mesh.shape["blk"], mesh.shape["partner"]),
        mesh=mesh, in_specs=placed, out_specs=P("blk", "partner", None), check_vma=False,
    )
```
